32 devices in a mesh: head: 4 (over x, core), blk: 8 (over z, y).
Axes of the slice: x: 2, y: 2, z: 4, core: 2. Of those that a mesh axis runs over, the one named last changes fastest.
Arguments:
- query: bfloat16 [4096, 4096], P(('blk', 'head')), may hold values from -6 to 6
- keys: bfloat16 [4096, 1024], P(('blk', 'head')), may hold values from -6 to 6
- values: bfloat16 [4096, 1024], P(('blk', 'head')), may hold values from -6 to 6
- forward_out: bfloat16 [4096, 4096], P(('blk', 'head')), may hold values from -6 to 6
- out_grad: bfloat16 [4096, 4096], P(('blk', 'head')), may hold values from -6 to 6
- log_norm: float32 [32, 4096], P(None, ('blk', 'head')), may hold values from 3 to 5
- tile_mask: int32 [8, 4, 4, 4], P('blk'), may hold values 0 or 1
Outputs:
- query_grad: bfloat16 [4096, 4096], P(('blk', 'head'))
- keys_grad: bfloat16 [4096, 1024], P(('blk', 'head'))
- values_grad: bfloat16 [4096, 1024], P(('blk', 'head'))
The draws below stay inside these ranges and needn't reach their ends.
All inputs are finite; a program needn't handle non-finite values. No bound on the sum of `tile_mask` on one device may be relied on, other than what follows from the above.
Results may differ from the reference program's by a relative error of at most 0.005.
Values may be sent and summed in bfloat16 or wider, within the bound.
No kernel may reach another device: no remote copies, remote signals or barrier semaphores. Data moves between devices by JAX's collectives and lax.ppermute only.
A program may use at most 128 MiB of HBM per device.

```python
import jax
import jax.numpy as jnp
from jax import lax

QH = 32
KH = 8
HD = 128
TILE = 128
STEPS = 4
TOK = 512
TT = 4
NBLK = 8
TOKENS = 4096
N_BLK = 8


def set_ends(result, key, smallest, top_value):
    extent = result.shape
    place = [jax.random.randint(jax.random.fold_in(key, axis), (), 0, extent[axis]) for axis in range(len(extent))]
    result = result.at[tuple(place)].set(smallest)
    longest = extent.index(max(extent))
    place[longest] = (place[longest] + 1) % extent[longest]
    return result.at[tuple(place)].set(top_value)


def block_levels(rng, shape, pieces, low, largest):
    factor_of = 1.0
    for dim, parts in pieces:
        draws = jax.random.uniform(jax.random.fold_in(jax.random.fold_in(rng, 6), dim), (parts,), jnp.float32, low / len(pieces), largest / len(pieces))
        factor_of = factor_of * jnp.repeat(jnp.exp(draws), shape[dim] // parts).reshape((-1,) + (1,) * (len(shape) - 1 - dim))
    return factor_of


def scatter_about(rng, dims, spread, most, split=(), kind=jnp.bfloat16):
    drawn = spread * jax.random.normal(rng, dims, jnp.float32)
    if split:
        drawn = drawn * block_levels(rng, dims, split, -0.22, 0.18)
    return jnp.clip(drawn, -most, most).astype(kind)


def setup_inputs(seed: int = 0) -> dict:
    key_list = jax.random.split(jax.random.key(seed), 8)
    query = scatter_about(key_list[0], (TOKENS, QH * HD), 1.0, 6.0, ((0, 32),))
    keys = scatter_about(key_list[1], (TOKENS, KH * HD), 1.0, 6.0, ((0, 32),))
    values = scatter_about(key_list[2], (TOKENS, KH * HD), 1.0, 6.0, ((0, 32),))
    forward_out = scatter_about(key_list[3], (TOKENS, QH * HD), 1.0, 6.0, ((0, 32),))
    out_grad = scatter_about(key_list[4], (TOKENS, QH * HD), 1.0, 6.0, ((0, 32),))
    log_norm = jnp.clip(3.0 + 2.0 * jax.random.uniform(key_list[5], (QH, TOKENS), jnp.float32) ** block_levels(key_list[5], (QH, TOKENS), ((1, 32),), -0.2, 0.2), 3.0, 5.0)
    tile_mask = set_ends((jax.random.randint(key_list[6], (NBLK, STEPS, TT, TT), 0, 2) < 1).astype(jnp.int32), jax.random.fold_in(key_list[6], 1), 0, 1)
    return {"query": query, "keys": keys, "values": values, "forward_out": forward_out, "out_grad": out_grad, "log_norm": log_norm, "tile_mask": tile_mask}


def expand_mask(tiles):
    width = tiles.shape[-1]
    seen = tiles[:, None, :, None] > 0
    seen = jnp.broadcast_to(seen, (width, TILE, width, TILE))
    return seen.reshape(width * TILE, width * TILE)


def block_terms(items):
    query_blk, keys_blk, values_blk, grad_blk, delta_blk, norm_blk, mask_blk = items
    scale = HD ** -0.5
    query_f = query_blk.astype(jnp.float32)
    keys_f = keys_blk.astype(jnp.float32)
    values_f = values_blk.astype(jnp.float32)
    grad_f = grad_blk.astype(jnp.float32)
    score = jnp.einsum('qkgd,pkd->kgqp', query_f, keys_f) * scale
    seen = expand_mask(mask_blk)
    prob = jnp.where(seen[None, None], jnp.exp(score - norm_blk[:, :, :, None]), jnp.float32(0.0))
    prob_b = lax.optimization_barrier(prob.astype(jnp.bfloat16)).astype(jnp.float32)
    values_term = jnp.einsum('kgqp,qkgd->pkd', prob_b, grad_f)
    dprob = jnp.einsum('qkgd,pkd->kgqp', grad_f, values_f)
    dscore = lax.optimization_barrier((prob * (dprob - delta_blk[:, :, :, None])).astype(jnp.bfloat16)).astype(jnp.float32)
    query_term = jnp.einsum('kgqp,pkd->qkgd', dscore, keys_f) * scale
    keys_term = jnp.einsum('kgqp,qkgd->pkd', dscore, query_f) * scale
    return query_term, keys_term, values_term


def reference(query, keys, values, forward_out, out_grad, log_norm, tile_mask):
    groups = QH // KH
    blocks = N_BLK
    query_b = query.reshape(blocks, TOK, KH, groups, HD)
    keys_b = keys.reshape(blocks, TOK, KH, HD)
    values_b = values.reshape(blocks, TOK, KH, HD)
    grad_b = out_grad.reshape(blocks, TOK, KH, groups, HD)
    delta = jnp.sum(out_grad.astype(jnp.float32).reshape(blocks, TOK, QH, HD) * forward_out.astype(jnp.float32).reshape(blocks, TOK, QH, HD), axis=-1)
    delta_b = jnp.transpose(delta, (0, 2, 1)).reshape(blocks, KH, groups, TOK)
    norm_b = jnp.transpose(log_norm.reshape(KH, groups, blocks, TOK), (2, 0, 1, 3))
    query_acc = jnp.zeros((blocks, TOK, KH, groups, HD), jnp.float32)
    keys_acc = jnp.zeros((blocks, TOK, KH, HD), jnp.float32)
    values_acc = jnp.zeros((blocks, TOK, KH, HD), jnp.float32)
    for step in range(STEPS):
        keys_s = jnp.roll(keys_b, step, axis=0)
        values_s = jnp.roll(values_b, step, axis=0)
        query_term, keys_term, values_term = lax.map(block_terms, (query_b, keys_s, values_s, grad_b, delta_b, norm_b, tile_mask[:, step]))
        query_acc = query_acc + query_term
        keys_acc = keys_acc + jnp.roll(keys_term, -step, axis=0)
        values_acc = values_acc + jnp.roll(values_term, -step, axis=0)
    total = blocks * TOK
    return (query_acc.reshape(total, QH * HD).astype(jnp.bfloat16),
            keys_acc.reshape(total, KH * HD).astype(jnp.bfloat16),
            values_acc.reshape(total, KH * HD).astype(jnp.bfloat16))
```

```python
import functools

import jax
import jax.numpy as jnp
from jax import lax
from jax.experimental import pallas as pl
from jax.experimental.pallas import tpu as pltpu
from jax.sharding import Mesh
from jax.sharding import PartitionSpec as P

HD = 128
STEPS = 4
SCALE = HD ** (-0.5)
LOG2E = 1.4426950408889634
F32 = jnp.float32
BF16 = jnp.bfloat16
EXTRA = 32
UNROLL = 4
PIPELINED = False
VMEM_LIMIT = 16 * 1024 * 1024
VMEM_ALL = 60 * 1024 * 1024

WHOLE = pl.BlockSpec(memory_space=pltpu.VMEM)
ANYWHERE = pl.BlockSpec(memory_space=pl.ANY)
SCALARS = pl.BlockSpec(memory_space=pltpu.SMEM)


def dot(a, b, dims):
    return lax.dot_general(a, b, (dims, ((), ())), preferred_element_type=F32)


def pack_kv(keys, values, tile_mask, parts):
    tokens = keys.shape[0]
    steps, tiles = tile_mask.shape[1:3]

    def kernel(k_ref, v_ref, m_ref, out_ref, mask):
        mask[...] = jnp.zeros_like(mask)
        for step in range(steps):
            mask[step * tiles : (step + 1) * tiles, :tiles] = m_ref[0, step].astype(F32)
        for g in range(parts):
            out_ref[g, :tokens, :] = k_ref[:, g * HD : (g + 1) * HD]
            out_ref[g, tokens : 2 * tokens, :] = v_ref[:, g * HD : (g + 1) * HD]
            out_ref[g, 2 * tokens :, :] = mask[...].astype(BF16)

    return pl.pallas_call(
        kernel,
        out_shape=jax.ShapeDtypeStruct((parts, 2 * tokens + steps * tiles, HD), keys.dtype),
        in_specs=[WHOLE, WHOLE, WHOLE],
        out_specs=WHOLE,
        scratch_shapes=[pltpu.VMEM((steps * tiles, HD), F32)],
        name="pack_kv",
    )(keys, values, tile_mask)


def split3(x):
    a = x.astype(BF16)
    r = x - a.astype(F32)
    b = r.astype(BF16)
    c = (r - b.astype(F32)).astype(BF16)
    return a, b, c


def pack_queries(me, query, out_grad, forward_out, log_norm, parts):
    tokens = query.shape[0]
    heads = log_norm.shape[0] // parts
    width = heads * HD
    rows = 2 * heads * tokens + EXTRA

    def kernel(me_ref, q_ref, g_ref, f_ref, n_ref, *refs):
        outs = refs[:parts]
        q_buf, g_buf, f_buf, n_buf, sem, n_sem = refs[parts:]
        n_load = pltpu.make_async_copy(n_ref, n_buf, n_sem)
        n_load.start()
        loads = []
        for d in range(parts):
            start = jnp.bitwise_xor(me_ref[0], d) * width
            lanes = pl.ds(pl.multiple_of(start, width), width)
            loads.append(
                [
                    pltpu.make_async_copy(ref.at[:, lanes], buf.at[d], sem.at[i, d])
                    for i, (ref, buf) in enumerate(((g_ref, g_buf), (f_ref, f_buf), (q_ref, q_buf)))
                ]
            )
            for copy in loads[d]:
                copy.start()
        line = lax.broadcasted_iota(jnp.int32, (16, width), 0)
        lane = lax.broadcasted_iota(jnp.int32, (16, width), 1)
        pick = jnp.where(lane // HD == line, 1.0, 0.0).astype(BF16)
        pad = jnp.zeros((EXTRA - 6 * heads, tokens), BF16)
        n_load.wait()
        for d, out in enumerate(outs):
            for copy in loads[d]:
                copy.wait()
            prod = g_buf[d].astype(F32) * f_buf[d].astype(F32)
            high = prod.astype(BF16)
            low = (prod - high.astype(F32)).astype(BF16)
            delta = (dot(pick, high, ((1,), (1,))) + dot(pick, low, ((1,), (1,))))[:heads]
            norm = n_buf[jnp.bitwise_xor(me_ref[0], d)]
            for h in range(heads):
                out[h * tokens : (h + 1) * tokens, :] = q_buf[d, :, h * HD : (h + 1) * HD]
                out[(heads + h) * tokens : (heads + h + 1) * tokens, :] = g_buf[d, :, h * HD : (h + 1) * HD]
            out[2 * heads * tokens :, :] = jnp.concatenate(split3(norm) + split3(delta) + (pad,), axis=0)

    return pl.pallas_call(
        kernel,
        out_shape=[jax.ShapeDtypeStruct((rows, HD), BF16)] * parts,
        in_specs=[SCALARS] + [ANYWHERE] * 4,
        out_specs=[WHOLE] * parts,
        scratch_shapes=[pltpu.VMEM((parts, tokens, width), BF16)] * 3
        + [
            pltpu.VMEM((parts, heads, tokens), F32),
            pltpu.SemaphoreType.DMA((3, parts)),
            pltpu.SemaphoreType.DMA,
        ],
        compiler_params=pltpu.CompilerParams(vmem_limit_bytes=VMEM_ALL),
        name="pack_queries",
    )(me, query, out_grad, forward_out, log_norm.reshape(parts, heads, tokens))


def side_by_side(x):
    return jnp.concatenate([x[h : h + 1] for h in range(x.shape[0])], axis=1)


def terms(where, masks, work, queries, kvs, dq_in, acc_in, dq_done, acc_done, tiles, heads):
    shards_in = [d for d, _ in work]
    names = [n for n in ("own", "one", "two") if any(n in use for _, use in work)]
    tokens = (queries[shards_in[0]].shape[0] - EXTRA) // (2 * heads)
    rows = heads * tokens
    dq_given = [d for d in shards_in if d in dq_in]
    acc_given = [n for n in names if n in acc_in]
    operands = [queries[d] for d in shards_in] + [kvs[n] for n in names]
    operands += [dq_in[d] for d in dq_given] + [acc_in[n] for n in acc_given]
    dq_shapes = [
        jax.ShapeDtypeStruct((rows, HD), BF16) if d in dq_done else jax.ShapeDtypeStruct((HD, rows), F32)
        for d in shards_in
    ]
    sizes = {n: kvs[n].shape[0] for n in names}
    starts = {n: sum(sizes[m] for m in names[:i]) for i, n in enumerate(names)}
    total = sum(sizes.values())
    acc_shapes = [jax.ShapeDtypeStruct((sizes[n], tokens, 2 * HD), BF16 if n in acc_done else F32) for n in names]
    longest = sum(2 * tiles * len(use) + UNROLL for _, use in work) + 4 * UNROLL
    block = UNROLL * tokens
    scratch = [
        pltpu.VMEM((len(work), 2 * rows, HD), BF16),
        pltpu.VMEM((len(work), 2, rows), F32),
        pltpu.VMEM((total, 2 * tokens, HD), BF16),
        pltpu.VMEM((total, tokens, 2 * HD), F32),
        pltpu.VMEM((len(work), HD, rows), F32),
        pltpu.SMEM((longest,), jnp.int32),
        pltpu.SMEM((longest,), F32),
        pltpu.SMEM((longest,), jnp.int32),
    ] + [pltpu.VMEM((block, rows), F32)] * (4 if PIPELINED else 0)

    def kernel(where_ref, mask_ref, *refs):
        refs = list(refs)
        take = lambda keys: {k: refs.pop(0) for k in keys}
        q_refs, kv_refs, dq_old, acc_old = take(shards_in), take(names), take(dq_given), take(acc_given)
        dq_out, acc_out = take(shards_in), take(names)
        q_buf, line_buf, kv_buf, acc, dq_acc, todo, penalty, shard_of = refs[:8]
        pair, head = where_ref[0], where_ref[1]
        for n in names:
            here = pl.ds(starts[n], sizes[n])
            kv_buf[here] = kv_refs[n][:, : 2 * tokens, :]
            acc[here] = acc_old[n][...] if n in acc_old else jnp.zeros((sizes[n], tokens, 2 * HD), F32)

        place = jnp.int32(0)
        for slot, (d, use) in enumerate(work):
            q_ref = q_refs[d]
            q_buf[slot] = q_ref[: 2 * rows, :]
            extra = q_ref[2 * rows :, :].astype(F32)
            piece = lambda k: extra[k * heads : (k + 1) * heads]
            line_buf[slot, 0:1, :] = side_by_side(piece(0) + piece(1) + piece(2)) * LOG2E
            line_buf[slot, 1:2, :] = side_by_side(piece(3) + piece(4) + piece(5))
            dq_acc[slot] = dq_old[d][...] if d in dq_old else jnp.zeros((HD, rows), F32)
            other = jnp.bitwise_xor(pair, d // tiles)
            row = jnp.bitwise_xor(head, d % tiles)

            def seen(step, j):
                return mask_ref[other, step * tiles * tiles + row * tiles + j]

            wanted = []
            if "own" in use:
                wanted += [(starts["own"] + j, seen(other, j)) for j in range(tiles)]
                wanted += [(starts["own"] + tiles + j, seen(0, j) * other) for j in range(tiles)]
            if "one" in use:
                wanted += [(starts["one"] + j, seen(2 + other, j)) for j in range(tiles)]
                wanted += [(starts["one"] + tiles + j, seen(1 + other, j)) for j in range(tiles)]
            if "two" in use:
                wanted += [(starts["two"] + j, seen(3, j) * (1 - other)) for j in range(tiles)]
            begin = place
            for tile, flag in wanted:
                todo[place] = jnp.int32(tile)
                penalty[place] = 0.0
                place = place + flag
            for u in range(UNROLL - 1):
                todo[place + u] = jnp.int32(0)
                penalty[place + u] = 1e30
            place = begin + (place - begin + UNROLL - 1) // UNROLL * UNROLL
            for g in range((len(wanted) + UNROLL - 1) // UNROLL):
                shard_of[begin // UNROLL + g] = jnp.int32(slot)
        groups = place // UNROLL
        for u in range(2 * UNROLL):
            todo[place + u] = jnp.int32(0)
            penalty[place + u] = 1e30
        shard_of[groups] = jnp.int32(0)
        shard_of[groups + 1] = jnp.int32(0)

        def load(g):
            slot = shard_of[g]
            spots = [todo[g * UNROLL + u] for u in range(UNROLL)]
            k = jnp.concatenate([kv_buf[t, :tokens, :] for t in spots], axis=0)
            return slot, spots, k

        def before(g):
            slot, spots, k = load(g)
            v = jnp.concatenate([kv_buf[t, tokens:, :] for t in spots], axis=0)
            return dot(k, q_buf[slot, :rows, :], ((1,), (1,))), dot(v, q_buf[slot, rows:, :], ((1,), (1,)))

        def after(g, score, dprob):
            slot, spots, k = load(g)
            lines = line_buf[slot]
            prob = jnp.concatenate(
                [
                    jnp.exp2(
                        score[u * tokens : (u + 1) * tokens] * (SCALE * LOG2E)
                        - (lines[0:1] + penalty[g * UNROLL + u])
                    )
                    for u in range(UNROLL)
                ],
                axis=0,
            )
            dscore = (prob * (dprob - lines[1:2])).astype(BF16)
            dv = dot(prob.astype(BF16), q_buf[slot, rows:, :], ((1,), (0,)))
            dk = dot(dscore, q_buf[slot, :rows, :], ((1,), (0,)))
            dq_acc[slot] += dot(k, dscore, ((0,), (0,)))
            for u, t in enumerate(spots):
                acc[t, :, :HD] += dk[u * tokens : (u + 1) * tokens]
                acc[t, :, HD:] += dv[u * tokens : (u + 1) * tokens]

        if PIPELINED:
            s0, p0, s1, p1 = refs[8:]
            s0[...], p0[...] = before(0)

            def body(i, carry):
                g = 2 * i
                s1[...], p1[...] = before(g + 1)
                after(g, s0[...], p0[...])
                s0[...], p0[...] = before(g + 2)
                after(g + 1, s1[...], p1[...])
                return carry

            lax.fori_loop(0, (groups + 1) // 2, body, 0)
        else:

            def body(g, carry):
                after(g, *before(g))
                return carry

            lax.fori_loop(0, groups, body, 0)

        for slot, d in enumerate(shards_in):
            if d in dq_done:
                dq_out[d][...] = (dq_acc[slot] * SCALE).T.astype(BF16)
            else:
                dq_out[d][...] = dq_acc[slot]
        for n in names:
            acc_out[n][...] = acc[pl.ds(starts[n], sizes[n])].astype(acc_out[n].dtype)

    outs = pl.pallas_call(
        kernel,
        out_shape=dq_shapes + acc_shapes,
        in_specs=[SCALARS, SCALARS] + [WHOLE] * len(operands),
        out_specs=[WHOLE] * (len(dq_shapes) + len(names)),
        scratch_shapes=scratch,
        compiler_params=pltpu.CompilerParams(vmem_limit_bytes=VMEM_LIMIT),
        cost_estimate=pl.CostEstimate(
            flops=10 * sum(len(use) for _, use in work) * rows * tiles * tokens * HD,
            bytes_accessed=sum(x.size * 2 for x in operands),
            transcendentals=0,
        ),
        name="terms",
    )(where, masks, *operands)
    return dict(zip(shards_in, outs)), dict(zip(names, outs[len(shards_in) :]))


def total_kv(own, one, two, after):
    tiles = two.shape[0]

    def kernel(own_ref, one_ref, two_ref, *refs):
        out_ref = refs[-1]
        for t in range(2 * tiles):
            total = own_ref[t] + one_ref[t].astype(F32)
            if t >= tiles:
                total = total + two_ref[t - tiles].astype(F32)
            out_ref[t, :, :HD] = (total[:, :HD] * SCALE).astype(BF16)
            out_ref[t, :, HD:] = total[:, HD:].astype(BF16)

    return pl.pallas_call(
        kernel,
        out_shape=jax.ShapeDtypeStruct(own.shape, BF16),
        in_specs=[WHOLE] * 3 + [ANYWHERE] * len(after),
        out_specs=WHOLE,
        name="total_kv",
    )(own, one, two, *after)


def unpack_queries(me, grads, tokens):
    parts = len(grads)
    heads = grads[0].shape[0] // tokens
    width = heads * HD

    def kernel(me_ref, *refs):
        out = refs[parts]
        for d in range(parts):
            source = jnp.bitwise_xor(me_ref[0], d)
            for h in range(heads):
                out[:, pl.ds(pl.multiple_of(source * width + h * HD, HD), HD)] = refs[d][h * tokens : (h + 1) * tokens, :]

    return pl.pallas_call(
        kernel,
        out_shape=jax.ShapeDtypeStruct((tokens, parts * width), BF16),
        in_specs=[SCALARS] + [WHOLE] * parts,
        out_specs=WHOLE,
        name="unpack_queries",
    )(me, *grads)


def unpack_kv(grads):
    parts, tokens = grads.shape[:2]

    def kernel(in_ref, k_ref, v_ref):
        for g in range(parts):
            k_ref[:, g * HD : (g + 1) * HD] = in_ref[g, :, :HD]
            v_ref[:, g * HD : (g + 1) * HD] = in_ref[g, :, HD:]

    return pl.pallas_call(
        kernel,
        out_shape=[jax.ShapeDtypeStruct((tokens, parts * HD), BF16)] * 2,
        in_specs=[WHOLE],
        out_specs=[WHOLE] * 2,
        name="unpack_kv",
    )(grads)


def shards(sizes, query, keys, values, forward_out, out_grad, log_norm, tile_mask):
    n_head, n_sup, n_pair = sizes
    parts = n_head * n_pair
    tiles = tile_mask.shape[-1]
    tokens = query.shape[0]
    heads = log_norm.shape[0] // parts
    pair, head = lax.axis_index("pair"), lax.axis_index("head")
    me = (pair * n_head + head).astype(jnp.int32).reshape(1)
    where = jnp.stack([pair, head]).astype(jnp.int32)

    def swap(value, d):
        far, near = d // n_head, d % n_head
        pairs = [
            (h * n_pair + p, (h ^ near) * n_pair + (p ^ far)) for h in range(n_head) for p in range(n_pair)
        ]
        return lax.ppermute(value, ("head", "pair"), pairs)

    def along(value, steps):
        return lax.ppermute(value, "sup", [(i, (i + steps) % n_sup) for i in range(n_sup)])

    def exchange(value):
        return lax.all_to_all(value, ("pair", "head"), split_axis=0, concat_axis=0, tiled=True)

    kv_own = exchange(pack_kv(keys, values, tile_mask, parts))
    packed = pack_queries(me, query, out_grad, forward_out, log_norm, parts)
    first = [0, 1, 2, n_head]
    last = [parts - 2, parts - 1]
    middle = [d for d in range(parts) if d not in first + last]
    queries = {d: swap(packed[d], d) if d else packed[d] for d in first}
    held, kv_own = lax.optimization_barrier(([packed[d] for d in middle], kv_own))
    kvs = {"own": kv_own, "one": along(kv_own, 1), "two": along(kv_own[n_head:], 2)}
    queries.update({d: swap(x, d) for d, x in zip(middle, held)})
    held, arrived = lax.optimization_barrier(([packed[d] for d in last], [queries[d] for d in first[2:]]))
    queries.update(dict(zip(first[2:], arrived)))
    queries.update({d: swap(x, d) for d, x in zip(last, held)})
    masks = kv_own[::n_head, 2 * tokens :, :tiles].astype(jnp.int32).reshape(n_pair, -1)
    args = dict(tiles=tiles, heads=heads)
    call = lambda work, dq, acc, dq_done, acc_done: terms(
        where, masks, work, queries, kvs, dq, acc, dq_done, acc_done, **args
    )
    dq, sums = call([(d, ["own"]) for d in first], {}, {}, [], [])
    some, sums = call([(d, ["one"]) for d in first] + [(d, ["own", "one"]) for d in middle], dq, sums, [], [])
    dq.update(some)
    some, sums = call([(d, ["own", "one"]) for d in last], {}, sums, [], ["one"])
    dq.update(some)
    one = along(sums["one"], -1)
    grads, two = call([(d, ["two"]) for d in range(parts)], dq, {}, list(range(parts)), ["two"])
    two = along(two["two"], -2)
    grads = [swap(grads[d], d) if d else grads[d] for d in range(parts)]
    kv_grad = exchange(total_kv(sums["own"], one, two, grads[1:]))
    query_grad = unpack_queries(me, grads, tokens)
    keys_grad, values_grad = unpack_kv(kv_grad)
    return query_grad, keys_grad, values_grad


def solution(mesh):
    sizes = dict(mesh.shape)
    n_head, n_blk = sizes["head"], sizes["blk"]
    n_pair = 2
    devices = mesh.devices
    if tuple(mesh.axis_names) != ("head", "blk"):
        raise ValueError("mesh axes")
    n_sup = n_blk // n_pair
    finer = Mesh(devices.reshape(n_head, n_sup, n_pair), ("head", "sup", "pair"))
    tokens = P(("sup", "pair", "head"), None)
    in_specs = (tokens,) * 5 + (P(None, ("sup", "pair", "head")), P(("sup", "pair"), None, None, None))
    return jax.shard_map(
        functools.partial(shards, (n_head, n_sup, n_pair)),
        mesh=finer,
        in_specs=in_specs,
        out_specs=(tokens,) * 3,
        check_vma=False,
    )
```

```python
import functools

import jax
import jax.numpy as jnp
from jax import lax
from jax.experimental import pallas as pl
from jax.experimental.pallas import tpu as pltpu
from jax.sharding import Mesh
from jax.sharding import PartitionSpec as P

HD = 128
STEPS = 4
SCALE = HD ** (-0.5)
LOG2E = 1.4426950408889634
F32 = jnp.float32
BF16 = jnp.bfloat16
EXTRA = 32
VMEM_LIMIT = 16 * 1024 * 1024
VMEM_ALL = 60 * 1024 * 1024

WHOLE = pl.BlockSpec(memory_space=pltpu.VMEM)
ANYWHERE = pl.BlockSpec(memory_space=pl.ANY)
SCALARS = pl.BlockSpec(memory_space=pltpu.SMEM)


def dot(a, b, dims):
    return lax.dot_general(a, b, (dims, ((), ())), preferred_element_type=F32)


def pack_kv(keys, values, tile_mask, parts):
    tokens = keys.shape[0]
    steps, tiles = tile_mask.shape[1:3]

    def kernel(k_ref, v_ref, m_ref, out_ref, mask):
        mask[...] = jnp.zeros_like(mask)
        for step in range(steps):
            mask[step * tiles : (step + 1) * tiles, :tiles] = m_ref[0, step].astype(F32)
        for g in range(parts):
            out_ref[g, :tokens, :] = k_ref[:, g * HD : (g + 1) * HD]
            out_ref[g, tokens : 2 * tokens, :] = v_ref[:, g * HD : (g + 1) * HD]
            out_ref[g, 2 * tokens :, :] = mask[...].astype(BF16)

    return pl.pallas_call(
        kernel,
        out_shape=jax.ShapeDtypeStruct((parts, 2 * tokens + steps * tiles, HD), keys.dtype),
        in_specs=[WHOLE, WHOLE, WHOLE],
        out_specs=WHOLE,
        scratch_shapes=[pltpu.VMEM((steps * tiles, HD), F32)],
        name="pack_kv",
    )(keys, values, tile_mask)


def split3(x):
    a = x.astype(BF16)
    r = x - a.astype(F32)
    b = r.astype(BF16)
    c = (r - b.astype(F32)).astype(BF16)
    return a, b, c


def pack_queries(me, query, out_grad, forward_out, log_norm, parts, offsets):
    tokens = query.shape[0]
    heads = log_norm.shape[0] // parts
    width = heads * HD
    rows = 2 * heads * tokens + EXTRA
    count = len(offsets)

    def kernel(me_ref, q_ref, g_ref, f_ref, n_ref, *refs):
        outs = refs[:count]
        q_buf, g_buf, f_buf, n_buf, sem, n_sem = refs[count:]
        n_load = pltpu.make_async_copy(n_ref, n_buf, n_sem)
        n_load.start()
        loads = []
        for s, d in enumerate(offsets):
            start = jnp.bitwise_xor(me_ref[0], d) * width
            lanes = pl.ds(pl.multiple_of(start, width), width)
            loads.append(
                [
                    pltpu.make_async_copy(ref.at[:, lanes], buf.at[s], sem.at[i, s])
                    for i, (ref, buf) in enumerate(((g_ref, g_buf), (f_ref, f_buf), (q_ref, q_buf)))
                ]
            )
            for copy in loads[s]:
                copy.start()
        line = lax.broadcasted_iota(jnp.int32, (16, width), 0)
        lane = lax.broadcasted_iota(jnp.int32, (16, width), 1)
        pick = jnp.where(lane // HD == line, 1.0, 0.0).astype(BF16)
        pad = jnp.zeros((EXTRA - 6 * heads, tokens), BF16)
        n_load.wait()
        for s, (d, out) in enumerate(zip(offsets, outs)):
            for copy in loads[s]:
                copy.wait()
            prod = g_buf[s].astype(F32) * f_buf[s].astype(F32)
            high = prod.astype(BF16)
            low = (prod - high.astype(F32)).astype(BF16)
            delta = (dot(pick, high, ((1,), (1,))) + dot(pick, low, ((1,), (1,))))[:heads]
            norm = n_buf[jnp.bitwise_xor(me_ref[0], d)]
            for h in range(heads):
                out[h * tokens : (h + 1) * tokens, :] = q_buf[s, :, h * HD : (h + 1) * HD]
                out[(heads + h) * tokens : (heads + h + 1) * tokens, :] = g_buf[s, :, h * HD : (h + 1) * HD]
            out[2 * heads * tokens :, :] = jnp.concatenate(split3(norm) + split3(delta) + (pad,), axis=0)

    return pl.pallas_call(
        kernel,
        out_shape=[jax.ShapeDtypeStruct((rows, HD), BF16)] * count,
        in_specs=[SCALARS] + [ANYWHERE] * 4,
        out_specs=[WHOLE] * count,
        scratch_shapes=[pltpu.VMEM((count, tokens, width), BF16)] * 3
        + [
            pltpu.VMEM((parts, heads, tokens), F32),
            pltpu.SemaphoreType.DMA((3, count)),
            pltpu.SemaphoreType.DMA,
        ],
        compiler_params=pltpu.CompilerParams(vmem_limit_bytes=VMEM_ALL),
        name="pack_queries",
    )(me, query, out_grad, forward_out, log_norm.reshape(parts, heads, tokens))


def side_by_side(x):
    return jnp.concatenate([x[h : h + 1] for h in range(x.shape[0])], axis=1)


def terms(where, masks, work, queries, kvs, dq_in, acc_in, dq_done, acc_done, unroll, tiles, heads):
    shards_in = [d for d, _ in work]
    names = [n for n in ("own", "one", "two") if any(n in use for _, use in work)]
    tokens = (queries[shards_in[0]].shape[0] - EXTRA) // (2 * heads)
    rows = heads * tokens
    dq_given = [d for d in shards_in if d in dq_in]
    acc_given = [n for n in names if n in acc_in]
    operands = [queries[d] for d in shards_in] + [kvs[n] for n in names]
    operands += [dq_in[d] for d in dq_given] + [acc_in[n] for n in acc_given]
    dq_shapes = [
        jax.ShapeDtypeStruct((rows, HD), BF16) if d in dq_done else jax.ShapeDtypeStruct((HD, rows), F32)
        for d in shards_in
    ]
    sizes = {n: kvs[n].shape[0] for n in names}
    starts = {n: sum(sizes[m] for m in names[:i]) for i, n in enumerate(names)}
    total = sum(sizes.values())
    acc_shapes = [jax.ShapeDtypeStruct((sizes[n], tokens, 2 * HD), BF16 if n in acc_done else F32) for n in names]
    longest = sum(2 * tiles * len(use) + unroll for _, use in work) + unroll
    scratch = [
        pltpu.VMEM((len(work), 2 * rows, HD), BF16),
        pltpu.VMEM((len(work), 2, rows), F32),
        pltpu.VMEM((total, 2 * tokens, HD), BF16),
        pltpu.VMEM((total, tokens, 2 * HD), F32),
        pltpu.VMEM((len(work), HD, rows), F32),
    ] + [pltpu.SMEM((longest,), jnp.int32)] * 3

    def kernel(where_ref, mask_ref, *refs):
        refs = list(refs)
        take = lambda keys: {k: refs.pop(0) for k in keys}
        q_refs, kv_refs, dq_old, acc_old = take(shards_in), take(names), take(dq_given), take(acc_given)
        dq_out, acc_out = take(shards_in), take(names)
        q_buf, line_buf, kv_buf, acc, dq_acc, todo, shard_of, end_of = refs
        pair, head = where_ref[0], where_ref[1]
        for n in names:
            here = pl.ds(starts[n], sizes[n])
            kv_buf[here] = kv_refs[n][:, : 2 * tokens, :]
            acc[here] = acc_old[n][...] if n in acc_old else jnp.zeros((sizes[n], tokens, 2 * HD), F32)

        place = jnp.int32(0)
        for slot, (d, use) in enumerate(work):
            q_ref = q_refs[d]
            q_buf[slot] = q_ref[: 2 * rows, :]
            extra = q_ref[2 * rows :, :].astype(F32)
            piece = lambda k: extra[k * heads : (k + 1) * heads]
            line_buf[slot, 0:1, :] = side_by_side(piece(0) + piece(1) + piece(2)) * LOG2E
            line_buf[slot, 1:2, :] = side_by_side(piece(3) + piece(4) + piece(5))
            dq_acc[slot] = dq_old[d][...] if d in dq_old else jnp.zeros((HD, rows), F32)
            other = jnp.bitwise_xor(pair, d // tiles)
            row = jnp.bitwise_xor(head, d % tiles)

            def seen(step, j):
                return mask_ref[other, step * tiles * tiles + row * tiles + j]

            wanted = []
            if "own" in use:
                wanted += [(starts["own"] + j, seen(other, j)) for j in range(tiles)]
                wanted += [(starts["own"] + tiles + j, seen(0, j) * other) for j in range(tiles)]
            if "one" in use:
                wanted += [(starts["one"] + j, seen(2 + other, j)) for j in range(tiles)]
                wanted += [(starts["one"] + tiles + j, seen(1 + other, j)) for j in range(tiles)]
            if "two" in use:
                wanted += [(starts["two"] + j, seen(3, j) * (1 - other)) for j in range(tiles)]
            begin = place
            for tile, flag in wanted:
                todo[place] = jnp.int32(tile)
                place = place + flag
            for u in range(unroll - 1):
                todo[place + u] = jnp.int32(0)
            for g in range((len(wanted) + unroll - 1) // unroll):
                shard_of[begin // unroll + g] = jnp.int32(slot)
                end_of[begin // unroll + g] = place
            place = begin + (place - begin + unroll - 1) // unroll * unroll

        def body(g, carry):
            slot = shard_of[g]
            spots = [todo[g * unroll + u] for u in range(unroll)]
            q, grad = q_buf[slot, :rows, :], q_buf[slot, rows:, :]
            k = jnp.concatenate([kv_buf[t, :tokens, :] for t in spots], axis=0)
            v = jnp.concatenate([kv_buf[t, tokens:, :] for t in spots], axis=0)
            lines = line_buf[slot]
            score = dot(k, q, ((1,), (1,)))
            dprob = dot(v, grad, ((1,), (1,)))
            prob = []
            for u in range(unroll):
                nothing = jnp.where(g * unroll + u < end_of[g], jnp.float32(0.0), jnp.float32(1e30))
                part = score[u * tokens : (u + 1) * tokens] * (SCALE * LOG2E)
                prob.append(jnp.exp2(part - (lines[0:1] + nothing)))
            prob = jnp.concatenate(prob, axis=0)
            dscore = (prob * (dprob - lines[1:2])).astype(BF16)
            dv = dot(prob.astype(BF16), grad, ((1,), (0,)))
            dk = dot(dscore, q, ((1,), (0,)))
            dq_acc[slot] += dot(k, dscore, ((0,), (0,)))
            for u, t in enumerate(spots):
                acc[t, :, :HD] += dk[u * tokens : (u + 1) * tokens]
                acc[t, :, HD:] += dv[u * tokens : (u + 1) * tokens]
            return carry

        lax.fori_loop(0, place // unroll, body, 0)

        for slot, d in enumerate(shards_in):
            if d in dq_done:
                dq_out[d][...] = (dq_acc[slot] * SCALE).T.astype(BF16)
            else:
                dq_out[d][...] = dq_acc[slot]
        for n in names:
            acc_out[n][...] = acc[pl.ds(starts[n], sizes[n])].astype(acc_out[n].dtype)

    outs = pl.pallas_call(
        kernel,
        out_shape=dq_shapes + acc_shapes,
        in_specs=[SCALARS, SCALARS] + [WHOLE] * len(operands),
        out_specs=[WHOLE] * (len(dq_shapes) + len(names)),
        scratch_shapes=scratch,
        compiler_params=pltpu.CompilerParams(vmem_limit_bytes=VMEM_LIMIT),
        cost_estimate=pl.CostEstimate(
            flops=10 * sum(len(use) for _, use in work) * rows * tiles * tokens * HD,
            bytes_accessed=sum(x.size * 2 for x in operands),
            transcendentals=0,
        ),
        name="terms",
    )(where, masks, *operands)
    return dict(zip(shards_in, outs)), dict(zip(names, outs[len(shards_in) :]))


def total_kv(own, one, two):
    lane = lax.broadcasted_iota(jnp.int32, (1, 1, 2 * HD), 2)
    lower = jnp.zeros_like(two)
    total = own + one.astype(F32) + jnp.concatenate([lower, two], axis=0).astype(F32)
    return (total * jnp.where(lane < HD, F32(SCALE), F32(1.0))).astype(BF16)


def unpack_queries(me, grads, tokens):
    parts = len(grads)
    heads = grads[0].shape[0] // tokens
    width = heads * HD

    def kernel(me_ref, *refs):
        out = refs[parts]
        for d in range(parts):
            source = jnp.bitwise_xor(me_ref[0], d)
            for h in range(heads):
                out[:, pl.ds(pl.multiple_of(source * width + h * HD, HD), HD)] = refs[d][h * tokens : (h + 1) * tokens, :]

    return pl.pallas_call(
        kernel,
        out_shape=jax.ShapeDtypeStruct((tokens, parts * width), BF16),
        in_specs=[SCALARS] + [WHOLE] * parts,
        out_specs=WHOLE,
        name="unpack_queries",
    )(me, *grads)


def unpack_kv(grads):
    parts, tokens = grads.shape[:2]
    lines = lambda x: x.transpose(1, 0, 2).reshape(tokens, parts * HD)
    return lines(grads[:, :, :HD]), lines(grads[:, :, HD:])


def shards(sizes, query, keys, values, forward_out, out_grad, log_norm, tile_mask):
    n_head, n_sup, n_pair = sizes
    parts = n_head * n_pair
    tiles = tile_mask.shape[-1]
    tokens = query.shape[0]
    heads = log_norm.shape[0] // parts
    pair, head = lax.axis_index("pair"), lax.axis_index("head")
    me = (pair * n_head + head).astype(jnp.int32).reshape(1)
    where = jnp.stack([pair, head]).astype(jnp.int32)

    def swap(value, d):
        far, near = d // n_head, d % n_head
        pairs = [
            (h * n_pair + p, (h ^ near) * n_pair + (p ^ far)) for h in range(n_head) for p in range(n_pair)
        ]
        return lax.ppermute(value, ("head", "pair"), pairs)

    def along(value, steps):
        return lax.ppermute(value, "sup", [(i, (i + steps) % n_sup) for i in range(n_sup)])

    def exchange(value):
        return lax.all_to_all(value, ("pair", "head"), split_axis=0, concat_axis=0, tiled=True)

    kv_own = exchange(pack_kv(keys, values, tile_mask, parts))
    first = [0, 1, 2, n_head]
    last = [parts - 2, parts - 1]
    middle = [d for d in range(parts) if d not in first + last]
    packed = {}
    for some in (first + middle, [d for d in range(parts) if d not in first + middle]):
        packed.update(zip(some, pack_queries(me, query, out_grad, forward_out, log_norm, parts, some)))
    queries = {d: swap(packed[d], d) if d else packed[d] for d in first + middle}
    queries[1], kv_own = lax.optimization_barrier((queries[1], kv_own))
    kvs = {"own": kv_own, "one": along(kv_own, 1), "two": along(kv_own[n_head:], 2)}
    held, arrived = lax.optimization_barrier(([packed[d] for d in last], [queries[d] for d in first[2:]]))
    queries.update(dict(zip(first[2:], arrived)))
    queries.update({d: swap(x, d) for d, x in zip(last, held)})
    masks = kv_own[::n_head, 2 * tokens :, :tiles].astype(jnp.int32).reshape(n_pair, -1)
    args = dict(tiles=tiles, heads=heads)
    call = lambda work, dq, acc, dq_done, acc_done, unroll=4: terms(
        where, masks, work, queries, kvs, dq, acc, dq_done, acc_done, unroll, **args
    )
    rest = middle + last
    dq, sums = call([(d, ["own"]) for d in first], {}, {}, [], [])
    dq, one = call([(d, ["one"]) for d in first], dq, {}, [], [])
    sums.update(one)
    some, sums = call([(d, ["own", "one"]) for d in rest], {}, sums, [], ["one"])
    dq.update(some)
    one = along(sums["one"], -1)
    grads, two = call([(d, ["two"]) for d in range(parts)], dq, {}, list(range(parts)), ["two"], 2)
    two = along(two["two"], -2)
    grads = [swap(grads[d], d) if d else grads[d] for d in range(parts)]
    one, two, grads[1:] = lax.optimization_barrier((one, two, grads[1:]))
    kv_grad = exchange(total_kv(sums["own"], one, two))
    query_grad = unpack_queries(me, grads, tokens)
    keys_grad, values_grad = unpack_kv(kv_grad)
    return query_grad, keys_grad, values_grad


def solution(mesh):
    sizes = dict(mesh.shape)
    n_head, n_blk = sizes["head"], sizes["blk"]
    n_pair = 2
    devices = mesh.devices
    if tuple(mesh.axis_names) != ("head", "blk"):
        raise ValueError("mesh axes")
    n_sup = n_blk // n_pair
    finer = Mesh(devices.reshape(n_head, n_sup, n_pair), ("head", "sup", "pair"))
    tokens = P(("sup", "pair", "head"), None)
    in_specs = (tokens,) * 5 + (P(None, ("sup", "pair", "head")), P(("sup", "pair"), None, None, None))
    return jax.shard_map(
        functools.partial(shards, (n_head, n_sup, n_pair)),
        mesh=finer,
        in_specs=in_specs,
        out_specs=(tokens,) * 3,
        check_vma=False,
    )
```

```python
import functools

import jax
import jax.numpy as jnp
from jax import lax
from jax.experimental import pallas as pl
from jax.experimental.pallas import tpu as pltpu
from jax.sharding import Mesh
from jax.sharding import PartitionSpec as P

HD = 128
STEPS = 4
SCALE = HD ** (-0.5)
LOG2E = 1.4426950408889634
F32 = jnp.float32
BF16 = jnp.bfloat16
EXTRA = 32
VMEM_LIMIT = 16 * 1024 * 1024
VMEM_ALL = 60 * 1024 * 1024

WHOLE = pl.BlockSpec(memory_space=pltpu.VMEM)
ANYWHERE = pl.BlockSpec(memory_space=pl.ANY)
SCALARS = pl.BlockSpec(memory_space=pltpu.SMEM)


def dot(a, b, dims):
    return lax.dot_general(a, b, (dims, ((), ())), preferred_element_type=F32)


def pack_kv(keys, values, tile_mask, parts):
    tokens = keys.shape[0]
    steps, tiles = tile_mask.shape[1:3]

    def kernel(k_ref, v_ref, m_ref, out_ref, mask):
        mask[...] = jnp.zeros_like(mask)
        for step in range(steps):
            mask[step * tiles : (step + 1) * tiles, :tiles] = m_ref[0, step].astype(F32)
        for g in range(parts):
            out_ref[g, :tokens, :] = k_ref[:, g * HD : (g + 1) * HD]
            out_ref[g, tokens : 2 * tokens, :] = v_ref[:, g * HD : (g + 1) * HD]
            out_ref[g, 2 * tokens :, :] = mask[...].astype(BF16)

    return pl.pallas_call(
        kernel,
        out_shape=jax.ShapeDtypeStruct((parts, 2 * tokens + steps * tiles, HD), keys.dtype),
        in_specs=[WHOLE, WHOLE, WHOLE],
        out_specs=WHOLE,
        scratch_shapes=[pltpu.VMEM((steps * tiles, HD), F32)],
        name="pack_kv",
    )(keys, values, tile_mask)


def split3(x):
    a = x.astype(BF16)
    r = x - a.astype(F32)
    b = r.astype(BF16)
    c = (r - b.astype(F32)).astype(BF16)
    return a, b, c


def pack_queries(me, query, out_grad, forward_out, log_norm, parts, offsets):
    tokens = query.shape[0]
    heads = log_norm.shape[0] // parts
    width = heads * HD
    rows = 2 * heads * tokens + EXTRA
    count = len(offsets)

    def kernel(me_ref, q_ref, g_ref, f_ref, n_ref, *refs):
        outs = refs[:count]
        q_buf, g_buf, f_buf, n_buf, sem, n_sem = refs[count:]
        n_load = pltpu.make_async_copy(n_ref, n_buf, n_sem)
        n_load.start()
        loads = []
        for s, d in enumerate(offsets):
            start = jnp.bitwise_xor(me_ref[0], d) * width
            lanes = pl.ds(pl.multiple_of(start, width), width)
            loads.append(
                [
                    pltpu.make_async_copy(ref.at[:, lanes], buf.at[s], sem.at[i, s])
                    for i, (ref, buf) in enumerate(((g_ref, g_buf), (f_ref, f_buf), (q_ref, q_buf)))
                ]
            )
            for copy in loads[s]:
                copy.start()
        line = lax.broadcasted_iota(jnp.int32, (16, width), 0)
        lane = lax.broadcasted_iota(jnp.int32, (16, width), 1)
        pick = jnp.where(lane // HD == line, 1.0, 0.0).astype(BF16)
        pad = jnp.zeros((EXTRA - 6 * heads, tokens), BF16)
        n_load.wait()
        for s, (d, out) in enumerate(zip(offsets, outs)):
            for copy in loads[s]:
                copy.wait()
            prod = g_buf[s].astype(F32) * f_buf[s].astype(F32)
            high = prod.astype(BF16)
            low = (prod - high.astype(F32)).astype(BF16)
            delta = (dot(pick, high, ((1,), (1,))) + dot(pick, low, ((1,), (1,))))[:heads]
            norm = n_buf[jnp.bitwise_xor(me_ref[0], d)]
            for h in range(heads):
                out[h * tokens : (h + 1) * tokens, :] = q_buf[s, :, h * HD : (h + 1) * HD]
                out[(heads + h) * tokens : (heads + h + 1) * tokens, :] = g_buf[s, :, h * HD : (h + 1) * HD]
            out[2 * heads * tokens :, :] = jnp.concatenate(split3(norm) + split3(delta) + (pad,), axis=0)

    return pl.pallas_call(
        kernel,
        out_shape=[jax.ShapeDtypeStruct((rows, HD), BF16)] * count,
        in_specs=[SCALARS] + [ANYWHERE] * 4,
        out_specs=[WHOLE] * count,
        scratch_shapes=[pltpu.VMEM((count, tokens, width), BF16)] * 3
        + [
            pltpu.VMEM((parts, heads, tokens), F32),
            pltpu.SemaphoreType.DMA((3, count)),
            pltpu.SemaphoreType.DMA,
        ],
        compiler_params=pltpu.CompilerParams(vmem_limit_bytes=VMEM_ALL),
        name="pack_queries",
    )(me, query, out_grad, forward_out, log_norm.reshape(parts, heads, tokens))


def side_by_side(x):
    return jnp.concatenate([x[h : h + 1] for h in range(x.shape[0])], axis=1)


def terms(where, masks, work, queries, kvs, dq_in, acc_in, dq_done, acc_done, unroll, tiles, heads):
    shards_in = [d for d, _ in work]
    names = [n for n in ("own", "one", "two") if any(n in use for _, use in work)]
    tokens = (queries[shards_in[0]].shape[0] - EXTRA) // (2 * heads)
    rows = heads * tokens
    dq_given = [d for d in shards_in if d in dq_in]
    acc_given = [n for n in names if n in acc_in]
    operands = [queries[d] for d in shards_in] + [kvs[n] for n in names]
    operands += [dq_in[d] for d in dq_given] + [acc_in[n] for n in acc_given]
    dq_shapes = [
        jax.ShapeDtypeStruct((rows, HD), BF16) if d in dq_done else jax.ShapeDtypeStruct((HD, rows), F32)
        for d in shards_in
    ]
    sizes = {n: kvs[n].shape[0] for n in names}
    starts = {n: sum(sizes[m] for m in names[:i]) for i, n in enumerate(names)}
    total = sum(sizes.values())
    acc_shapes = [jax.ShapeDtypeStruct((sizes[n], tokens, 2 * HD), BF16 if n in acc_done else F32) for n in names]
    longest = sum(2 * tiles * len(use) + unroll for _, use in work) + unroll
    scratch = [
        pltpu.VMEM((len(work), 2 * rows, HD), BF16),
        pltpu.VMEM((len(work), 2, rows), F32),
        pltpu.VMEM((total, 2 * tokens, HD), BF16),
        pltpu.VMEM((total, tokens, 2 * HD), F32),
        pltpu.VMEM((len(work), HD, rows), F32),
    ] + [pltpu.SMEM((longest,), jnp.int32)] * 3

    def kernel(where_ref, mask_ref, *refs):
        refs = list(refs)
        take = lambda keys: {k: refs.pop(0) for k in keys}
        q_refs, kv_refs, dq_old, acc_old = take(shards_in), take(names), take(dq_given), take(acc_given)
        dq_out, acc_out = take(shards_in), take(names)
        q_buf, line_buf, kv_buf, acc, dq_acc, todo, shard_of, end_of = refs
        pair, head = where_ref[0], where_ref[1]
        for n in names:
            here = pl.ds(starts[n], sizes[n])
            kv_buf[here] = kv_refs[n][:, : 2 * tokens, :]
            acc[here] = acc_old[n][...] if n in acc_old else jnp.zeros((sizes[n], tokens, 2 * HD), F32)

        place = jnp.int32(0)
        for slot, (d, use) in enumerate(work):
            q_ref = q_refs[d]
            q_buf[slot] = q_ref[: 2 * rows, :]
            extra = q_ref[2 * rows :, :].astype(F32)
            piece = lambda k: extra[k * heads : (k + 1) * heads]
            line_buf[slot, 0:1, :] = side_by_side(piece(0) + piece(1) + piece(2)) * LOG2E
            line_buf[slot, 1:2, :] = side_by_side(piece(3) + piece(4) + piece(5))
            dq_acc[slot] = dq_old[d][...] if d in dq_old else jnp.zeros((HD, rows), F32)
            other = jnp.bitwise_xor(pair, d // tiles)
            row = jnp.bitwise_xor(head, d % tiles)

            def seen(step, j):
                return mask_ref[other, step * tiles * tiles + row * tiles + j]

            wanted = []
            if "own" in use:
                wanted += [(starts["own"] + j, seen(other, j)) for j in range(tiles)]
                wanted += [(starts["own"] + tiles + j, seen(0, j) * other) for j in range(tiles)]
            if "one" in use:
                wanted += [(starts["one"] + j, seen(2 + other, j)) for j in range(tiles)]
                wanted += [(starts["one"] + tiles + j, seen(1 + other, j)) for j in range(tiles)]
            if "two" in use:
                wanted += [(starts["two"] + j, seen(3, j) * (1 - other)) for j in range(tiles)]
            begin = place
            for tile, flag in wanted:
                todo[place] = jnp.int32(tile)
                place = place + flag
            for u in range(unroll - 1):
                todo[place + u] = jnp.int32(0)
            for g in range((len(wanted) + unroll - 1) // unroll):
                shard_of[begin // unroll + g] = jnp.int32(slot)
                end_of[begin // unroll + g] = place
            place = begin + (place - begin + unroll - 1) // unroll * unroll

        def body(g, carry):
            slot = shard_of[g]
            spots = [todo[g * unroll + u] for u in range(unroll)]
            q, grad = q_buf[slot, :rows, :], q_buf[slot, rows:, :]
            k = jnp.concatenate([kv_buf[t, :tokens, :] for t in spots], axis=0)
            v = jnp.concatenate([kv_buf[t, tokens:, :] for t in spots], axis=0)
            lines = line_buf[slot]
            score = dot(k, q, ((1,), (1,)))
            dprob = dot(v, grad, ((1,), (1,)))
            prob = []
            for u in range(unroll):
                nothing = jnp.where(g * unroll + u < end_of[g], jnp.float32(0.0), jnp.float32(1e30))
                part = score[u * tokens : (u + 1) * tokens] * (SCALE * LOG2E)
                prob.append(jnp.exp2(part - (lines[0:1] + nothing)))
            prob = jnp.concatenate(prob, axis=0)
            dscore = (prob * (dprob - lines[1:2])).astype(BF16)
            dv = dot(prob.astype(BF16), grad, ((1,), (0,)))
            dk = dot(dscore, q, ((1,), (0,)))
            dq_acc[slot] += dot(k, dscore, ((0,), (0,)))
            for u, t in enumerate(spots):
                acc[t, :, :HD] += dk[u * tokens : (u + 1) * tokens]
                acc[t, :, HD:] += dv[u * tokens : (u + 1) * tokens]
            return carry

        lax.fori_loop(0, place // unroll, body, 0)

        for slot, d in enumerate(shards_in):
            if d in dq_done:
                dq_out[d][...] = (dq_acc[slot] * SCALE).T.astype(BF16)
            else:
                dq_out[d][...] = dq_acc[slot]
        for n in names:
            acc_out[n][...] = acc[pl.ds(starts[n], sizes[n])].astype(acc_out[n].dtype)

    outs = pl.pallas_call(
        kernel,
        out_shape=dq_shapes + acc_shapes,
        in_specs=[SCALARS, SCALARS] + [WHOLE] * len(operands),
        out_specs=[WHOLE] * (len(dq_shapes) + len(names)),
        scratch_shapes=scratch,
        compiler_params=pltpu.CompilerParams(vmem_limit_bytes=VMEM_LIMIT),
        cost_estimate=pl.CostEstimate(
            flops=10 * sum(len(use) for _, use in work) * rows * tiles * tokens * HD,
            bytes_accessed=sum(x.size * 2 for x in operands),
            transcendentals=0,
        ),
        name="terms",
    )(where, masks, *operands)
    return dict(zip(shards_in, outs)), dict(zip(names, outs[len(shards_in) :]))


def total_kv(own, one, two):
    lane = lax.broadcasted_iota(jnp.int32, (1, 1, 2 * HD), 2)
    lower = jnp.zeros_like(two)
    total = own + one.astype(F32) + jnp.concatenate([lower, two], axis=0).astype(F32)
    return (total * jnp.where(lane < HD, F32(SCALE), F32(1.0))).astype(BF16)


def unpack_queries(me, grads, tokens):
    parts = len(grads)
    heads = grads[0].shape[0] // tokens
    width = heads * HD

    def kernel(me_ref, *refs):
        out = refs[parts]
        for d in range(parts):
            source = jnp.bitwise_xor(me_ref[0], d)
            for h in range(heads):
                out[:, pl.ds(pl.multiple_of(source * width + h * HD, HD), HD)] = refs[d][h * tokens : (h + 1) * tokens, :]

    return pl.pallas_call(
        kernel,
        out_shape=jax.ShapeDtypeStruct((tokens, parts * width), BF16),
        in_specs=[SCALARS] + [WHOLE] * parts,
        out_specs=WHOLE,
        compiler_params=pltpu.CompilerParams(vmem_limit_bytes=VMEM_LIMIT),
        name="unpack_queries",
    )(me, *grads)


def unpack_kv(grads):
    parts, tokens = grads.shape[:2]

    def kernel(in_ref, k_ref, v_ref):
        for g in range(parts):
            k_ref[:, g * HD : (g + 1) * HD] = in_ref[g, :, :HD]
            v_ref[:, g * HD : (g + 1) * HD] = in_ref[g, :, HD:]

    return pl.pallas_call(
        kernel,
        out_shape=[jax.ShapeDtypeStruct((tokens, parts * HD), BF16)] * 2,
        in_specs=[WHOLE],
        out_specs=[WHOLE] * 2,
        compiler_params=pltpu.CompilerParams(vmem_limit_bytes=VMEM_LIMIT),
        name="unpack_kv",
    )(grads)


def shards(sizes, query, keys, values, forward_out, out_grad, log_norm, tile_mask):
    n_head, n_sup, n_pair = sizes
    parts = n_head * n_pair
    tiles = tile_mask.shape[-1]
    tokens = query.shape[0]
    heads = log_norm.shape[0] // parts
    pair, head = lax.axis_index("pair"), lax.axis_index("head")
    me = (pair * n_head + head).astype(jnp.int32).reshape(1)
    where = jnp.stack([pair, head]).astype(jnp.int32)

    def swap(value, d):
        far, near = d // n_head, d % n_head
        pairs = [
            (h * n_pair + p, (h ^ near) * n_pair + (p ^ far)) for h in range(n_head) for p in range(n_pair)
        ]
        return lax.ppermute(value, ("head", "pair"), pairs)

    def along(value, steps):
        return lax.ppermute(value, "sup", [(i, (i + steps) % n_sup) for i in range(n_sup)])

    def exchange(value):
        return lax.all_to_all(value, ("pair", "head"), split_axis=0, concat_axis=0, tiled=True)

    kv_own = exchange(pack_kv(keys, values, tile_mask, parts))
    first = [0, 1, 2, n_head]
    last = [parts - 2, parts - 1]
    middle = [d for d in range(parts) if d not in first + last]
    packed = {}
    for some in (first + middle, [d for d in range(parts) if d not in first + middle]):
        packed.update(zip(some, pack_queries(me, query, out_grad, forward_out, log_norm, parts, some)))
    queries = {d: swap(packed[d], d) if d else packed[d] for d in first + middle}
    queries[1], kv_own = lax.optimization_barrier((queries[1], kv_own))
    kvs = {"own": kv_own, "one": along(kv_own, 1), "two": along(kv_own[n_head:], 2)}
    held, arrived = lax.optimization_barrier(([packed[d] for d in last], [queries[d] for d in first[2:]]))
    queries.update(dict(zip(first[2:], arrived)))
    queries.update({d: swap(x, d) for d, x in zip(last, held)})
    masks = kv_own[::n_head, 2 * tokens :, :tiles].astype(jnp.int32).reshape(n_pair, -1)
    args = dict(tiles=tiles, heads=heads)
    call = lambda work, dq, acc, dq_done, acc_done, unroll=4: terms(
        where, masks, work, queries, kvs, dq, acc, dq_done, acc_done, unroll, **args
    )
    rest = middle + last
    dq, sums = call([(d, ["own"]) for d in first], {}, {}, [], [])
    dq, one = call([(d, ["one"]) for d in first], dq, {}, [], [])
    sums.update(one)
    some, sums = call([(d, ["own", "one"]) for d in rest], {}, sums, [], ["one"])
    dq.update(some)
    one = along(sums["one"], -1)
    grads, two = call([(d, ["two"]) for d in range(parts)], dq, {}, list(range(parts)), ["two"], 2)
    two = along(two["two"], -2)
    grads = [swap(grads[d], d) if d else grads[d] for d in range(parts)]
    one, two, grads[1:] = lax.optimization_barrier((one, two, grads[1:]))
    kv_grad = exchange(total_kv(sums["own"], one, two))
    query_grad = unpack_queries(me, grads, tokens)
    keys_grad, values_grad = unpack_kv(kv_grad)
    return query_grad, keys_grad, values_grad


def solution(mesh):
    sizes = dict(mesh.shape)
    n_head, n_blk = sizes["head"], sizes["blk"]
    n_pair = 2
    devices = mesh.devices
    if tuple(mesh.axis_names) != ("head", "blk"):
        raise ValueError("mesh axes")
    n_sup = n_blk // n_pair
    finer = Mesh(devices.reshape(n_head, n_sup, n_pair), ("head", "sup", "pair"))
    tokens = P(("sup", "pair", "head"), None)
    in_specs = (tokens,) * 5 + (P(None, ("sup", "pair", "head")), P(("sup", "pair"), None, None, None))
    return jax.shard_map(
        functools.partial(shards, (n_head, n_sup, n_pair)),
        mesh=finer,
        in_specs=in_specs,
        out_specs=(tokens,) * 3,
        check_vma=False,
    )
```

```python
import functools

import jax
import jax.numpy as jnp
from jax import lax
from jax.experimental import pallas as pl
from jax.experimental.pallas import tpu as pltpu
from jax.sharding import Mesh
from jax.sharding import PartitionSpec as P

HD = 128
STEPS = 4
SCALE = HD ** (-0.5)
LOG2E = 1.4426950408889634
F32 = jnp.float32
BF16 = jnp.bfloat16
EXTRA = 16
VMEM_LIMIT = 16 * 1024 * 1024
VMEM_ALL = 60 * 1024 * 1024

WHOLE = pl.BlockSpec(memory_space=pltpu.VMEM)
ANYWHERE = pl.BlockSpec(memory_space=pl.ANY)
SCALARS = pl.BlockSpec(memory_space=pltpu.SMEM)


def dot(a, b, dims):
    return lax.dot_general(a, b, (dims, ((), ())), preferred_element_type=F32)


def pack_kv(keys, values, tile_mask, parts):
    tokens = keys.shape[0]
    steps, tiles = tile_mask.shape[1:3]

    def kernel(k_ref, v_ref, m_ref, out_ref, mask):
        mask[...] = jnp.zeros_like(mask)
        for step in range(steps):
            mask[step * tiles : (step + 1) * tiles, :tiles] = m_ref[0, step].astype(F32)
        for g in range(parts):
            out_ref[g, :tokens, :] = k_ref[:, g * HD : (g + 1) * HD]
            out_ref[g, tokens : 2 * tokens, :] = v_ref[:, g * HD : (g + 1) * HD]
            out_ref[g, 2 * tokens :, :] = mask[...].astype(BF16)

    return pl.pallas_call(
        kernel,
        out_shape=jax.ShapeDtypeStruct((parts, 2 * tokens + steps * tiles, HD), keys.dtype),
        in_specs=[WHOLE, WHOLE, WHOLE],
        out_specs=WHOLE,
        scratch_shapes=[pltpu.VMEM((steps * tiles, HD), F32)],
        name="pack_kv",
    )(keys, values, tile_mask)


def split2(x):
    a = x.astype(BF16)
    return a, (x - a.astype(F32)).astype(BF16)


def pack_queries(me, query, out_grad, forward_out, log_norm, parts, offsets):
    tokens = query.shape[0]
    heads = log_norm.shape[0] // parts
    width = heads * HD
    rows = 2 * heads * tokens + EXTRA
    count = len(offsets)

    def kernel(me_ref, q_ref, g_ref, f_ref, n_ref, *refs):
        outs = refs[:count]
        q_buf, g_buf, f_buf, n_buf, sem, n_sem = refs[count:]
        n_load = pltpu.make_async_copy(n_ref, n_buf, n_sem)
        n_load.start()
        loads = []
        for s, d in enumerate(offsets):
            start = jnp.bitwise_xor(me_ref[0], d) * width
            lanes = pl.ds(pl.multiple_of(start, width), width)
            loads.append(
                [
                    pltpu.make_async_copy(ref.at[:, lanes], buf.at[s], sem.at[i, s])
                    for i, (ref, buf) in enumerate(((g_ref, g_buf), (f_ref, f_buf), (q_ref, q_buf)))
                ]
            )
            for copy in loads[s]:
                copy.start()
        line = lax.broadcasted_iota(jnp.int32, (16, width), 0)
        lane = lax.broadcasted_iota(jnp.int32, (16, width), 1)
        pick = jnp.where(lane // HD == line, 1.0, 0.0).astype(BF16)
        n_load.wait()
        for s, (d, out) in enumerate(zip(offsets, outs)):
            for copy in loads[s]:
                copy.wait()
            prod = g_buf[s].astype(F32) * f_buf[s].astype(F32)
            high = prod.astype(BF16)
            low = (prod - high.astype(F32)).astype(BF16)
            delta = (dot(pick, high, ((1,), (1,))) + dot(pick, low, ((1,), (1,))))[:heads]
            norm = n_buf[jnp.bitwise_xor(me_ref[0], d)]
            for h in range(heads):
                out[h * tokens : (h + 1) * tokens, :] = q_buf[s, :, h * HD : (h + 1) * HD]
                out[(heads + h) * tokens : (heads + h + 1) * tokens, :] = g_buf[s, :, h * HD : (h + 1) * HD]
            out[2 * heads * tokens :, :] = jnp.concatenate(split2(norm) + split2(delta), axis=0)

    return pl.pallas_call(
        kernel,
        out_shape=[jax.ShapeDtypeStruct((rows, HD), BF16)] * count,
        in_specs=[SCALARS] + [ANYWHERE] * 4,
        out_specs=[WHOLE] * count,
        scratch_shapes=[pltpu.VMEM((count, tokens, width), BF16)] * 3
        + [
            pltpu.VMEM((parts, heads, tokens), F32),
            pltpu.SemaphoreType.DMA((3, count)),
            pltpu.SemaphoreType.DMA,
        ],
        compiler_params=pltpu.CompilerParams(vmem_limit_bytes=VMEM_ALL),
        name="pack_queries",
    )(me, query, out_grad, forward_out, log_norm.reshape(parts, heads, tokens))


def side_by_side(x):
    return jnp.concatenate([x[h : h + 1] for h in range(x.shape[0])], axis=1)


def terms(where, masks, work, queries, kvs, dq_in, acc_in, dq_done, acc_done, unroll, tiles, heads):
    shards_in = [d for d, _ in work]
    names = [n for n in ("own", "one", "two") if any(n in use for _, use in work)]
    tokens = (queries[shards_in[0]].shape[0] - EXTRA) // (2 * heads)
    rows = heads * tokens
    dq_given = [d for d in shards_in if d in dq_in]
    acc_given = [n for n in names if n in acc_in]
    operands = [queries[d] for d in shards_in] + [kvs[n] for n in names]
    operands += [dq_in[d] for d in dq_given] + [acc_in[n] for n in acc_given]
    dq_shapes = [
        jax.ShapeDtypeStruct((rows, HD), BF16) if d in dq_done else jax.ShapeDtypeStruct((HD, rows), F32)
        for d in shards_in
    ]
    sizes = {n: kvs[n].shape[0] for n in names}
    starts = {n: sum(sizes[m] for m in names[:i]) for i, n in enumerate(names)}
    total = sum(sizes.values())
    acc_shapes = [jax.ShapeDtypeStruct((sizes[n], tokens, 2 * HD), BF16 if n in acc_done else F32) for n in names]
    longest = sum(2 * tiles * len(use) + unroll for _, use in work) + unroll
    scratch = [
        pltpu.VMEM((len(work), 2 * rows, HD), BF16),
        pltpu.VMEM((len(work), 2, rows), F32),
        pltpu.VMEM((total, 2 * tokens, HD), BF16),
        pltpu.VMEM((total, tokens, 2 * HD), F32),
        pltpu.VMEM((len(work), HD, rows), F32),
    ] + [pltpu.SMEM((longest,), jnp.int32)] * 3

    def kernel(where_ref, mask_ref, *refs):
        refs = list(refs)
        take = lambda keys: {k: refs.pop(0) for k in keys}
        q_refs, kv_refs, dq_old, acc_old = take(shards_in), take(names), take(dq_given), take(acc_given)
        dq_out, acc_out = take(shards_in), take(names)
        q_buf, line_buf, kv_buf, acc, dq_acc, todo, shard_of, end_of = refs
        pair, head = where_ref[0], where_ref[1]
        for n in names:
            here = pl.ds(starts[n], sizes[n])
            kv_buf[here] = kv_refs[n][:, : 2 * tokens, :]
            acc[here] = acc_old[n][...] if n in acc_old else jnp.zeros((sizes[n], tokens, 2 * HD), F32)

        place = jnp.int32(0)
        for slot, (d, use) in enumerate(work):
            q_ref = q_refs[d]
            q_buf[slot] = q_ref[: 2 * rows, :]
            extra = q_ref[2 * rows :, :].astype(F32)
            piece = lambda k: extra[k * heads : (k + 1) * heads]
            line_buf[slot, 0:1, :] = side_by_side(piece(0) + piece(1)) * LOG2E
            line_buf[slot, 1:2, :] = side_by_side(piece(2) + piece(3))
            dq_acc[slot] = dq_old[d][...] if d in dq_old else jnp.zeros((HD, rows), F32)
            other = jnp.bitwise_xor(pair, d // tiles)
            row = jnp.bitwise_xor(head, d % tiles)

            def seen(step, j):
                return mask_ref[other, step * tiles * tiles + row * tiles + j]

            wanted = []
            if "own" in use:
                wanted += [(starts["own"] + j, seen(other, j)) for j in range(tiles)]
                wanted += [(starts["own"] + tiles + j, seen(0, j) * other) for j in range(tiles)]
            if "one" in use:
                wanted += [(starts["one"] + j, seen(2 + other, j)) for j in range(tiles)]
                wanted += [(starts["one"] + tiles + j, seen(1 + other, j)) for j in range(tiles)]
            if "two" in use:
                wanted += [(starts["two"] + j, seen(3, j) * (1 - other)) for j in range(tiles)]
            begin = place
            for tile, flag in wanted:
                todo[place] = jnp.int32(tile)
                place = place + flag
            for u in range(unroll - 1):
                todo[place + u] = jnp.int32(0)
            for g in range((len(wanted) + unroll - 1) // unroll):
                shard_of[begin // unroll + g] = jnp.int32(slot)
                end_of[begin // unroll + g] = place
            place = begin + (place - begin + unroll - 1) // unroll * unroll

        def body(g, carry):
            slot = shard_of[g]
            spots = [todo[g * unroll + u] for u in range(unroll)]
            q, grad = q_buf[slot, :rows, :], q_buf[slot, rows:, :]
            k = jnp.concatenate([kv_buf[t, :tokens, :] for t in spots], axis=0)
            v = jnp.concatenate([kv_buf[t, tokens:, :] for t in spots], axis=0)
            lines = line_buf[slot]
            score = dot(k, q, ((1,), (1,)))
            dprob = dot(v, grad, ((1,), (1,)))
            prob = []
            for u in range(unroll):
                nothing = jnp.where(g * unroll + u < end_of[g], jnp.float32(0.0), jnp.float32(1e30))
                part = score[u * tokens : (u + 1) * tokens] * (SCALE * LOG2E)
                prob.append(jnp.exp2(part - (lines[0:1] + nothing)))
            prob = jnp.concatenate(prob, axis=0)
            dscore = (prob * (dprob - lines[1:2])).astype(BF16)
            dv = dot(prob.astype(BF16), grad, ((1,), (0,)))
            dk = dot(dscore, q, ((1,), (0,)))
            dq_acc[slot] += dot(k, dscore, ((0,), (0,)))
            for u, t in enumerate(spots):
                acc[t, :, :HD] += dk[u * tokens : (u + 1) * tokens]
                acc[t, :, HD:] += dv[u * tokens : (u + 1) * tokens]
            return carry

        lax.fori_loop(0, place // unroll, body, 0)

        for slot, d in enumerate(shards_in):
            if d in dq_done:
                dq_out[d][...] = (dq_acc[slot] * SCALE).T.astype(BF16)
            else:
                dq_out[d][...] = dq_acc[slot]
        for n in names:
            acc_out[n][...] = acc[pl.ds(starts[n], sizes[n])].astype(acc_out[n].dtype)

    outs = pl.pallas_call(
        kernel,
        out_shape=dq_shapes + acc_shapes,
        in_specs=[SCALARS, SCALARS] + [WHOLE] * len(operands),
        out_specs=[WHOLE] * (len(dq_shapes) + len(names)),
        scratch_shapes=scratch,
        compiler_params=pltpu.CompilerParams(vmem_limit_bytes=VMEM_LIMIT),
        cost_estimate=pl.CostEstimate(
            flops=10 * sum(len(use) for _, use in work) * rows * tiles * tokens * HD,
            bytes_accessed=sum(x.size * 2 for x in operands),
            transcendentals=0,
        ),
        name="terms",
    )(where, masks, *operands)
    return dict(zip(shards_in, outs)), dict(zip(names, outs[len(shards_in) :]))


def total_kv(own, one, two):
    lane = lax.broadcasted_iota(jnp.int32, (1, 1, 2 * HD), 2)
    lower = jnp.zeros_like(two)
    total = own + one.astype(F32) + jnp.concatenate([lower, two], axis=0).astype(F32)
    return (total * jnp.where(lane < HD, F32(SCALE), F32(1.0))).astype(BF16)


def unpack_queries(me, grads, tokens):
    parts = len(grads)
    heads = grads[0].shape[0] // tokens
    width = heads * HD

    def kernel(me_ref, *refs):
        out = refs[parts]
        for d in range(parts):
            source = jnp.bitwise_xor(me_ref[0], d)
            for h in range(heads):
                out[:, pl.ds(pl.multiple_of(source * width + h * HD, HD), HD)] = refs[d][h * tokens : (h + 1) * tokens, :]

    return pl.pallas_call(
        kernel,
        out_shape=jax.ShapeDtypeStruct((tokens, parts * width), BF16),
        in_specs=[SCALARS] + [WHOLE] * parts,
        out_specs=WHOLE,
        compiler_params=pltpu.CompilerParams(vmem_limit_bytes=VMEM_LIMIT),
        name="unpack_queries",
    )(me, *grads)


def unpack_kv(grads):
    parts, tokens = grads.shape[:2]

    def kernel(in_ref, k_ref, v_ref):
        for g in range(parts):
            k_ref[:, g * HD : (g + 1) * HD] = in_ref[g, :, :HD]
            v_ref[:, g * HD : (g + 1) * HD] = in_ref[g, :, HD:]

    return pl.pallas_call(
        kernel,
        out_shape=[jax.ShapeDtypeStruct((tokens, parts * HD), BF16)] * 2,
        in_specs=[WHOLE],
        out_specs=[WHOLE] * 2,
        compiler_params=pltpu.CompilerParams(vmem_limit_bytes=VMEM_LIMIT),
        name="unpack_kv",
    )(grads)


def shards(sizes, query, keys, values, forward_out, out_grad, log_norm, tile_mask):
    n_head, n_sup, n_pair = sizes
    parts = n_head * n_pair
    tiles = tile_mask.shape[-1]
    tokens = query.shape[0]
    heads = log_norm.shape[0] // parts
    pair, head = lax.axis_index("pair"), lax.axis_index("head")
    me = (pair * n_head + head).astype(jnp.int32).reshape(1)
    where = jnp.stack([pair, head]).astype(jnp.int32)

    def swap(value, d):
        far, near = d // n_head, d % n_head
        pairs = [
            (h * n_pair + p, (h ^ near) * n_pair + (p ^ far)) for h in range(n_head) for p in range(n_pair)
        ]
        return lax.ppermute(value, ("head", "pair"), pairs)

    def along(value, steps):
        return lax.ppermute(value, "sup", [(i, (i + steps) % n_sup) for i in range(n_sup)])

    def exchange(value):
        return lax.all_to_all(value, ("pair", "head"), split_axis=0, concat_axis=0, tiled=True)

    kv_own = exchange(pack_kv(keys, values, tile_mask, parts))
    first = [0, 1, 2, n_head]
    last = [parts - 2, parts - 1]
    middle = [d for d in range(parts) if d not in first + last]
    packed = {}
    for some in (first + middle, [d for d in range(parts) if d not in first + middle]):
        packed.update(zip(some, pack_queries(me, query, out_grad, forward_out, log_norm, parts, some)))
    queries = {d: swap(packed[d], d) if d else packed[d] for d in first + middle}
    queries[1], kv_own = lax.optimization_barrier((queries[1], kv_own))
    kvs = {"own": kv_own, "one": along(kv_own, 1), "two": along(kv_own[n_head:], 2)}
    held, arrived = lax.optimization_barrier(([packed[d] for d in last], [queries[d] for d in first[2:]]))
    queries.update(dict(zip(first[2:], arrived)))
    queries.update({d: swap(x, d) for d, x in zip(last, held)})
    masks = kv_own[::n_head, 2 * tokens :, :tiles].astype(jnp.int32).reshape(n_pair, -1)
    args = dict(tiles=tiles, heads=heads)
    call = lambda work, dq, acc, dq_done, acc_done, unroll=4: terms(
        where, masks, work, queries, kvs, dq, acc, dq_done, acc_done, unroll, **args
    )
    rest = middle + last
    dq, sums = call([(d, ["own"]) for d in first], {}, {}, [], [])
    dq, one = call([(d, ["one"]) for d in first], dq, {}, [], [])
    sums.update(one)
    some, sums = call([(d, ["own", "one"]) for d in rest], {}, sums, [], ["one"])
    dq.update(some)
    one = along(sums["one"], -1)
    grads, two = call([(d, ["two"]) for d in range(parts)], dq, {}, list(range(parts)), ["two"], 2)
    two = along(two["two"], -2)
    grads = [swap(grads[d], d) if d else grads[d] for d in range(parts)]
    one, two, grads[1:] = lax.optimization_barrier((one, two, grads[1:]))
    kv_grad = exchange(total_kv(sums["own"], one, two))
    query_grad = unpack_queries(me, grads, tokens)
    keys_grad, values_grad = unpack_kv(kv_grad)
    return query_grad, keys_grad, values_grad


def solution(mesh):
    sizes = dict(mesh.shape)
    n_head, n_blk = sizes["head"], sizes["blk"]
    n_pair = 2
    devices = mesh.devices
    if tuple(mesh.axis_names) != ("head", "blk"):
        raise ValueError("mesh axes")
    n_sup = n_blk // n_pair
    finer = Mesh(devices.reshape(n_head, n_sup, n_pair), ("head", "sup", "pair"))
    tokens = P(("sup", "pair", "head"), None)
    in_specs = (tokens,) * 5 + (P(None, ("sup", "pair", "head")), P(("sup", "pair"), None, None, None))
    return jax.shard_map(
        functools.partial(shards, (n_head, n_sup, n_pair)),
        mesh=finer,
        in_specs=in_specs,
        out_specs=(tokens,) * 3,
        check_vma=False,
    )
```
